32 devices in a mesh: groups: 2 (over y), dp: 4 (over z), fsdp: 4 (over x, core).
Axes of the slice: x: 2, y: 2, z: 4, core: 2. Of those that a mesh axis runs over, the one named last changes fastest.
Arguments:
- tokens: bfloat16 [8192, 5120], P(('groups', 'dp', 'fsdp')), parts along dimension 0, may hold values from -6 to 6
- row_tenant_index: int32 [8192, 1], P(('groups', 'dp', 'fsdp')), parts along dimension 0, may hold values from 0 to 31; in each aligned block of 256 rows (0 to 255, 256 to 511, ...) at most 8 rows name the same one
- tenant_adapter_slot: int32 [32], replicated, may hold values from 0 to 31, each once
- live_row_counts: int32 [32], P(('groups', 'dp', 'fsdp')), parts along dimension 0, may hold values from 192 to 256
- readout: bfloat16 [8192, 1024], P(('groups', 'dp', 'fsdp')), parts along dimension 0, may hold values from -0.125 to 0.125
- advantage: bfloat16 [8192], P(('groups', 'dp', 'fsdp')), parts along dimension 0, may hold values from -6 to 6
- base_value_matrix: bfloat16 [5120, 1024], P('fsdp'), may hold values from -0.078125 to 0.078125
- adapter_down_maps: bfloat16 [32, 5120, 32], P('dp'), may hold values from -0.078125 to 0.078125
- adapter_up_maps: bfloat16 [32, 32, 1024], P('dp'), may hold values from -0.5 to 0.5
Outputs:
- values: bfloat16 [8192, 1024], P(('groups', 'dp', 'fsdp')), parts along dimension 0
- kl_rows: float32 [8192], P(('groups', 'dp', 'fsdp')), parts along dimension 0
- down_map_gradient: float32 [64, 5120, 32], P(('groups', 'dp'), 'fsdp'), parts along dimension 0
- up_map_gradient: float32 [64, 32, 1024], P(('groups', 'dp'), None, 'fsdp'), parts along dimension 0
The draws below stay inside these ranges and needn't reach their ends.
There are 2 independent parts, one for each index of `groups`. The reference program is written for one: setup_inputs(seed, part) draws one part's arguments, and reference() takes and returns one part's arrays. A program takes and returns all parts, laid end to end along the dimension named above; an argument that names none is the same for every part. Nothing has to cross between parts.
Inputs may be any that keep to these rules, and one draw needn't show every extreme that they name: `row_tenant_index`: within the rows of one device no tenant is named more than 8 times.
All inputs are finite; a program needn't handle non-finite values.
Results may differ from the reference program's by a relative error of at most 0.008.
Values may be sent and summed in bfloat16 or wider, within the bound.
A program may use at most 128 MiB of HBM per device.

```python
import math
import jax
import jax.numpy as jnp
import numpy as np
from jax import lax

MODEL_WIDTH = 5120
VALUE_WIDTH = 1024
ADAPTER_RANK = 32
ROWS_DEV = 256
MOST = 8
TENANT_SLOTS = 32
TOKENS = 4096
N_DP = 4
N_FSDP = 4


def draw_live_row_counts(key, part):
    key = jax.random.fold_in(key, 7)
    first, second = jax.random.split(key)
    number = N_DP * N_FSDP
    counts = jax.random.randint(first, (number,), 3 * ROWS_DEV // 4, ROWS_DEV + 1)
    order = jax.random.permutation(second, number)
    counts = counts.at[order[0]].set(ROWS_DEV)
    counts = counts.at[order[1]].set(3 * ROWS_DEV // 4)
    return counts.astype(jnp.int32)


def block_levels(rng, shape, shards, smallest, top_value):
    loudness, own = 1.0, jax.random.fold_in(rng, 6)
    for dim, blocks in shards:
        heights = jnp.exp(jax.random.uniform(jax.random.fold_in(own, dim), (blocks,), jnp.float32, smallest / len(shards), top_value / len(shards)))
        loudness = loudness * jnp.repeat(heights, shape[dim] // blocks).reshape([-1 if axis == dim else 1 for axis in range(len(shape))])
    return loudness


def shared_out(key, own, number, rows, amount, top, most, slope):
    order = jax.random.permutation(key, amount)
    packed, usual = portions_of(amount, rows * top, most, slope, True), portions_of(amount, rows * top, most, slope, False)
    places = jnp.arange(amount)

    def named(tallies, offset_by):
        used = int((tallies > 0).sum())
        fixed = max(1, used // 4)
        moved = fixed + (places - fixed + offset_by * (used - fixed)) % max(1, amount - fixed)
        return jnp.zeros((amount,), jnp.int32).at[order[jnp.where(places < fixed, places, moved)]].set(jnp.asarray(tallies, jnp.int32))

    tallies = jnp.where(number % 4 == 0, named(packed, number // 4), named(usual, number - number // 4 - 1))
    mixed = jax.random.permutation(jax.random.fold_in(own, 3), amount)
    source_of, sink = mixed[0:amount // 2 * 2:2], mixed[1:amount // 2 * 2:2]
    margin = jnp.minimum(tallies[source_of] - 1, most - tallies[sink]) // 2
    margin = jnp.where((source_of == order[0]) | (sink == order[0]) | (tallies[sink] == 0), 0, jnp.maximum(margin, 0))
    moved = jax.random.randint(jax.random.fold_in(own, 4), (amount // 2,), 0, 1 << 20) % (margin + 1)
    tallies = tallies.at[source_of].add(-moved).at[sink].add(moved)
    items = jnp.searchsorted(jnp.cumsum(tallies), jnp.arange(rows * top), side="right").astype(jnp.int32)
    grid = items.reshape(top, rows).T
    grid = grid[jax.random.permutation(jax.random.fold_in(own, 1), rows)]
    offset_by = jax.random.randint(jax.random.fold_in(own, 2), (rows, 1), 0, top)
    return jnp.take_along_axis(grid, (jnp.arange(top)[None, :] + offset_by) % top, axis=1)


def portions_of(amount, total, reach, lean, full):
    portions = [(1 << 20) // math.isqrt(standing ** lean) + 1 for standing in range(1, amount + 1)]
    largest = reach if full else min(reach, max(-(-total // amount), total * portions[0] // sum(portions)))
    least = 1 if total - largest >= amount - 1 else 0
    given, spare = [largest] + [least] * (amount - 1), total - largest - least * (amount - 1)
    while spare > 0:
        candidates = [i for i in range(1, amount) if given[i] < largest] or [i for i in range(1, amount) if given[i] < reach]
        whole, budget = sum([portions[i] for i in candidates]), spare
        for i in candidates:
            extra = min(reach - given[i], max(1, budget * portions[i] // whole), spare)
            given[i] = given[i] + extra
            spare = spare - extra
    return np.array(given)


def normal_values(rng, extent, spread, reach, cuts=(), held_as=jnp.bfloat16):
    values = jax.random.normal(rng, extent, jnp.float32) * spread
    if len(cuts) > 0:
        values = block_levels(rng, extent, cuts, -0.22, 0.18) * values
    return jnp.clip(values, min=-reach, max=reach).astype(held_as)


def setup_inputs(seed: int = 0, part: int = 0) -> dict:
    keys = jax.random.split(jax.random.key(seed), 10)
    own_keys = jax.random.split(jax.random.fold_in(keys[9], part), 10)
    tokens = normal_values(own_keys[0], (TOKENS, MODEL_WIDTH), 1.0, 6.0, ((0, 16),))
    row_tenant_index_keys = jax.random.split(jax.random.fold_in(own_keys[1], 1), TOKENS // ROWS_DEV)
    row_tenant_index_turns = jax.random.permutation(jax.random.fold_in(own_keys[1], 3), TOKENS // ROWS_DEV)
    row_tenant_index = jax.vmap(lambda own, number: shared_out(jax.random.fold_in(own_keys[1], 2), own, number, ROWS_DEV, TENANT_SLOTS, 1, MOST, 2))(row_tenant_index_keys, row_tenant_index_turns).reshape((TOKENS, 1))
    tenant_adapter_slot = jax.random.permutation(keys[2], TENANT_SLOTS).astype(jnp.int32)
    live_row_counts = draw_live_row_counts(jax.random.fold_in(jax.random.fold_in(keys[9], part), 71), part)
    readout = normal_values(own_keys[4], (TOKENS, VALUE_WIDTH), 0.02, 0.125, ((0, 16),))
    advantage = normal_values(own_keys[5], (TOKENS,), 1.0, 6.0, ((0, 16),))
    base_value_matrix = normal_values(keys[6], (MODEL_WIDTH, VALUE_WIDTH), MODEL_WIDTH ** -0.5, 0.078125, ((0, 4),))
    adapter_down_maps = normal_values(keys[7], (TENANT_SLOTS, MODEL_WIDTH, ADAPTER_RANK), MODEL_WIDTH ** -0.5, 0.078125, ((0, 4),))
    adapter_up_maps = normal_values(keys[8], (TENANT_SLOTS, ADAPTER_RANK, VALUE_WIDTH), (4 * ADAPTER_RANK) ** -0.5, 0.5, ((0, 4),))
    return {"tokens": tokens, "row_tenant_index": row_tenant_index, "tenant_adapter_slot": tenant_adapter_slot, "live_row_counts": live_row_counts, "readout": readout, "advantage": advantage, "base_value_matrix": base_value_matrix, "adapter_down_maps": adapter_down_maps, "adapter_up_maps": adapter_up_maps}


adapter_scale = 2.0
kl_weight = 0.5


def reference(tokens, row_tenant_index, tenant_adapter_slot, live_row_counts, readout, advantage, base_value_matrix, adapter_down_maps, adapter_up_maps):
    blocks = N_DP * N_FSDP
    slots = tenant_adapter_slot[row_tenant_index[:, 0]].astype(jnp.int32)
    xs = (tokens.reshape(blocks, ROWS_DEV, MODEL_WIDTH), slots.reshape(blocks, ROWS_DEV),
          readout.reshape(blocks, ROWS_DEV, VALUE_WIDTH), advantage.reshape(blocks, ROWS_DEV), live_row_counts)

    def step(loop_carried, item):
        rows, adapter_slot_index, direction, adv, count = item
        live = jnp.arange(ROWS_DEV, dtype=jnp.int32) < count
        base = jnp.dot(rows, base_value_matrix, preferred_element_type=jnp.float32)
        down_map_rows = adapter_down_maps[adapter_slot_index].astype(jnp.float32)
        up_map_rows = adapter_up_maps[adapter_slot_index].astype(jnp.float32)
        rows32 = rows.astype(jnp.float32)
        low = jnp.einsum('nd,ndr->nr', rows32, down_map_rows).astype(jnp.bfloat16)
        rank_projected_single = low.astype(jnp.float32)
        adapter_difference = (adapter_scale * jnp.einsum('to,tou->tu', rank_projected_single, up_map_rows)).astype(jnp.bfloat16)
        delta32 = jnp.where(live[:, None], adapter_difference.astype(jnp.float32), jnp.float32(0.0))
        values = (base + delta32).astype(jnp.bfloat16)
        dir32 = direction.astype(jnp.float32)
        gap = jnp.sum(delta32 * dir32, axis=1)
        kl = jnp.where(live, jnp.exp(-gap) + gap - 1.0, jnp.float32(0.0))
        coeff = jnp.where(live, kl_weight * (1.0 - jnp.exp(-gap)) - adv.astype(jnp.float32), jnp.float32(0.0))
        output_gradient = (coeff[:, None] * dir32).astype(jnp.bfloat16)
        output_gradient_single = output_gradient.astype(jnp.float32)
        rank_space_gradient = (adapter_scale * jnp.einsum('qw,qvw->qv', output_gradient_single, up_map_rows)).astype(jnp.bfloat16)
        down_map_gradient = loop_carried[0] + jax.ops.segment_sum(rows32[:, :, None] * rank_space_gradient.astype(jnp.float32)[:, None, :], adapter_slot_index, num_segments=TENANT_SLOTS)
        up_map_gradient = loop_carried[1] + adapter_scale * jax.ops.segment_sum(rank_projected_single[:, :, None] * output_gradient_single[:, None, :], adapter_slot_index, num_segments=TENANT_SLOTS)
        return (down_map_gradient, up_map_gradient), (values, kl)

    init = (jnp.zeros((TENANT_SLOTS, MODEL_WIDTH, ADAPTER_RANK), jnp.float32), jnp.zeros((TENANT_SLOTS, ADAPTER_RANK, VALUE_WIDTH), jnp.float32))
    (down_map_gradient, up_map_gradient), (values, kl) = lax.scan(step, init, xs)
    return values.reshape(TOKENS, VALUE_WIDTH), kl.reshape(TOKENS), down_map_gradient, up_map_gradient
```

```python
import functools

import jax
import jax.numpy as jnp
from jax import lax
from jax.experimental import pallas as pl
from jax.experimental.pallas import tpu as pltpu
from jax.sharding import PartitionSpec as P

MOST = 8

adapter_scale = 2.0
kl_weight = 0.5
bf16 = jnp.bfloat16
f32 = jnp.float32
LANES = 128


def rounded(a):
    return lax.reduce_precision(a.astype(f32), 8, 7).astype(bf16)


def nt(a, b):
    return lax.dot_general(a, b, (((1,), (1,)), ((), ())), preferred_element_type=f32)


def tn(a, b):
    return lax.dot_general(a, b, (((0,), (0,)), ((), ())), preferred_element_type=f32)


def adapters_kernel(
    owners, shares, rank,
    pick_ref, tokens_ref, readout_ref, adv_ref, down_ref, up_ref,
    delta_ref, kl_ref, down_grad_ref, up_grad_ref,
    x_send, x_recv, low_send, low_recv, up_all, m_send, m_recv, dirs,
    xs, xr, ls, lr, ms, mr, us, ur, vs, vr,
):
    peers = owners * shares
    d, f = lax.axis_index("dp"), lax.axis_index("fsdp")
    me = d * shares + f
    buffer_rows, rows = pick_ref.shape
    block = buffer_rows // owners
    wide = up_ref.shape[0]
    part = tokens_ref.shape[1] // shares
    cut = readout_ref.shape[1] // shares

    def where_is(p):
        return {"dp": p // shares, "fsdp": lax.rem(p, shares)}

    def copy(src, dst, send, recv, p):
        return pltpu.make_async_remote_copy(
            src_ref=src, dst_ref=dst, send_sem=send, recv_sem=recv,
            device_id=where_is(p), device_id_type=pl.DeviceIdType.MESH,
        )

    def x_copy(to, source):
        return copy(x_send.at[to], x_recv.at[source], xs.at[to], xr.at[source], to)

    def low_copy(to, source):
        return copy(low_send.at[to], low_recv.at[source], ls.at[to], lr.at[source], to)

    def m_copy(to, source):
        return copy(m_send.at[to], m_recv.at[source], ms.at[to], mr.at[source], to)

    def other(k):
        return lax.rem(me + k, peers)

    barrier = pltpu.get_barrier_semaphore()
    for k in range(1, peers):
        pl.semaphore_signal(
            barrier, inc=1, device_id=where_is(other(k)), device_id_type=pl.DeviceIdType.MESH
        )
    pl.semaphore_wait(barrier, peers - 1)

    my_cut = pl.ds(pl.multiple_of(f * cut, LANES), cut)

    def up_copy(to_d, source):
        return copy(up_ref.at[:, my_cut], up_all.at[f, source], us.at[to_d], ur.at[source], to_d * shares + f)

    for j in range(1, owners):
        up_copy(lax.rem(d + j, owners), d).start()
    up_all[f, d] = up_ref[:, my_cut]

    for i in range(shares):
        s = lax.rem(f + i, shares)
        columns = pl.ds(pl.multiple_of(s * part, LANES), part)
        moved = jnp.dot(pick_ref[...], tokens_ref[:, columns], preferred_element_type=f32).astype(bf16)
        for o in range(owners):
            x_send[o * shares + s] = moved[o * block : (o + 1) * block]
        for j in range(owners):
            o = lax.rem(d + owners // 2 + j, owners)
            if i == 0 and j == owners - owners // 2:
                continue
            x_copy(o * shares + s, me).start()
    x_recv[me] = x_send[me]

    def up_on(to_f, source):
        return copy(up_all.at[f], up_all.at[source], vs.at[to_f], vr.at[source], d * shares + to_f)

    for j in range(1, owners):
        up_copy(d, lax.rem(d + j, owners)).wait_recv()
    for j in range(1, shares):
        s = lax.rem(f + j, shares)
        copy(up_all.at[f], up_all.at[f], vs.at[s], vr.at[f], d * shares + s).start()

    dirs[...] = jnp.dot(pick_ref[...], readout_ref[...], preferred_element_type=f32)
    hit = pick_ref[...].astype(f32) > 0.5
    adv = jnp.sum(jnp.where(hit, adv_ref[...], 0.0), axis=1, keepdims=True)

    my_part = pl.ds(pl.multiple_of(f * part, LANES), part)
    own = (
        lax.broadcasted_iota(jnp.int32, (block, wide), 0) // MOST
        == lax.broadcasted_iota(jnp.int32, (block, wide), 1) // rank
    )

    def low_of(q):
        every = jnp.where(own, nt(x_recv[q], down_ref[:, my_part]), 0.0)
        total = every[:, :LANES]
        for g in range(1, wide // LANES):
            total = total + every[:, g * LANES : (g + 1) * LANES]
        return total

    low_recv[me] = low_of(me)

    def step(k, carry):
        q = lax.rem(me + k, peers)
        x_copy(q, q).wait_recv()
        low_send[q] = low_of(q)
        low_copy(q, me).start()
        return carry

    lax.fori_loop(1, peers, step, 0)

    for j in range(1, shares):
        up_on(f, lax.rem(f + j, shares)).wait_recv()

    for k in range(1, peers):
        low_copy(other(k), other(k)).wait_recv()
    blocks = []
    for o in range(owners):
        total = low_recv[o * shares]
        for s in range(1, shares):
            total = total + low_recv[o * shares + s]
        blocks.append(total)
    low = jnp.concatenate(blocks, axis=0).astype(bf16)
    low32 = low.astype(f32)
    columns = owners * wide
    mine = (
        lax.broadcasted_iota(jnp.int32, (buffer_rows, columns), 0) // MOST
        == lax.broadcasted_iota(jnp.int32, (buffer_rows, columns), 1) // rank
    )
    spread = jnp.where(mine, jnp.concatenate([low32] * (columns // LANES), axis=1), 0.0).astype(bf16)
    deltas = []
    gap = jnp.zeros((buffer_rows, 1), f32)
    for s in range(shares):
        up = up_all[s].reshape(columns, cut)
        delta = (adapter_scale * jnp.dot(spread, up, preferred_element_type=f32)).astype(bf16)
        deltas.append(delta)
        gap = gap + jnp.sum(delta.astype(f32) * dirs[:, s * cut : (s + 1) * cut], axis=1, keepdims=True)
    small = jnp.exp(-gap)
    coeff = kl_weight * (1.0 - small) - adv
    back = jnp.zeros((buffer_rows, columns), f32)
    for s in range(shares):
        cot = (coeff * dirs[:, s * cut : (s + 1) * cut]).astype(bf16)
        for o in range(owners):
            m_send[o * shares + s, :, LANES:] = cot[o * block : (o + 1) * block]
        back = back + nt(cot, up_all[s].reshape(columns, cut))
    back = jnp.where(mine, back, 0.0)
    total = back[:, :LANES]
    for g in range(1, columns // LANES):
        total = total + back[:, g * LANES : (g + 1) * LANES]
    packed = (adapter_scale * total + pltpu.roll(low32, LANES // 2, 1)).astype(bf16)
    for o in range(owners):
        for s in range(shares):
            m_send[o * shares + s, :, :LANES] = packed[o * block : (o + 1) * block]
    for k in range(1, peers):
        m_copy(other(k), me).start()
    m_recv[me] = m_send[me]

    kl_ref[...] = jnp.sum(jnp.where(hit, small + gap - 1.0, 0.0), axis=0, keepdims=True)
    for s in range(shares):
        delta_ref[:, s * cut : (s + 1) * cut] = tn(pick_ref[...], deltas[s]).astype(bf16)

    for k in range(1, peers):
        m_copy(other(k), other(k)).wait_recv()
    got = m_recv[:, :, :LANES].reshape(peers * block, LANES).astype(f32)
    chosen = (
        lax.rem(lax.broadcasted_iota(jnp.int32, (peers * block, wide), 0), block) // MOST
        == lax.broadcasted_iota(jnp.int32, (peers * block, wide), 1) // rank
    )

    def widened(a):
        return jnp.where(chosen, jnp.concatenate([a] * (wide // LANES), axis=1), 0.0).astype(bf16)

    grad_wide = widened(got)
    low_wide = widened(pltpu.roll(got, LANES // 2, 1))
    for c in range(0, part, 256):
        down_grad_ref[:, c : c + 256] = tn(
            grad_wide, x_recv[:, :, c : c + 256].reshape(peers * block, 256)
        )
    up_grad_ref[...] = adapter_scale * tn(low_wide, m_recv[:, :, LANES:].reshape(peers * block, cut))

    for j in range(1, owners):
        up_copy(lax.rem(d + j, owners), d).wait_send()
    for j in range(1, shares):
        s = lax.rem(f + j, shares)
        copy(up_all.at[f], up_all.at[f], vs.at[s], vr.at[f], d * shares + s).wait_send()
    for k in range(1, peers):
        x_copy(other(k), me).wait_send()
        low_copy(other(k), me).wait_send()
        m_copy(other(k), me).wait_send()


def adapters(pick, tokens, readout, adv, down, up, owners, shares, rank):
    buffer_rows, rows = pick.shape
    width, proj = tokens.shape[1], readout.shape[1]
    wide = up.shape[0]
    peers, block = owners * shares, buffer_rows // owners
    part, cut = width // shares, proj // shares
    dma = pltpu.SemaphoreType.DMA
    return pl.pallas_call(
        functools.partial(adapters_kernel, owners, shares, rank),
        out_shape=(
            jax.ShapeDtypeStruct((rows, proj), bf16),
            jax.ShapeDtypeStruct((1, rows), f32),
            jax.ShapeDtypeStruct((wide, part), f32),
            jax.ShapeDtypeStruct((wide, cut), f32),
        ),
        in_specs=[pl.BlockSpec(memory_space=pltpu.VMEM)] * 6,
        out_specs=tuple([pl.BlockSpec(memory_space=pltpu.VMEM)] * 4),
        scratch_shapes=[
            pltpu.VMEM((peers, block, part), bf16),
            pltpu.VMEM((peers, block, part), bf16),
            pltpu.VMEM((peers, block, LANES), f32),
            pltpu.VMEM((peers, block, LANES), f32),
            pltpu.VMEM((shares, owners, wide, cut), bf16),
            pltpu.VMEM((peers, block, LANES + cut), bf16),
            pltpu.VMEM((peers, block, LANES + cut), bf16),
            pltpu.VMEM((buffer_rows, proj), f32),
        ]
        + [dma((peers,))] * 6
        + [dma((owners,))] * 2
        + [dma((shares,))] * 2,
        compiler_params=pltpu.CompilerParams(
            collective_id=0, has_side_effects=True, vmem_limit_bytes=48 * 1024 * 1024
        ),
        cost_estimate=pl.CostEstimate(
            flops=8 * 10**9, bytes_accessed=12 * 2**20, transcendentals=buffer_rows
        ),
    )(pick, tokens, readout, adv, down, up)


def per_device(
    tokens,
    row_tenant_index,
    tenant_adapter_slot,
    live_row_counts,
    readout,
    advantage,
    base_value_matrix,
    adapter_down_maps,
    adapter_up_maps,
):
    rows, width = tokens.shape
    proj = base_value_matrix.shape[1]
    owners = lax.axis_size("dp")
    shares = lax.axis_size("fsdp")
    local, _, rank = adapter_down_maps.shape
    slots = tenant_adapter_slot.shape[0]
    per_owner = local * MOST
    buffer_rows = owners * per_owner
    peers = owners * shares
    part = width // shares
    proj_part = proj // shares
    both = ("dp", "fsdp")
    share = lax.axis_index("fsdp")

    base_all = lax.all_gather(base_value_matrix, "fsdp", axis=0, tiled=True)

    number = jnp.arange(rows, dtype=jnp.int32)
    live = number < live_row_counts[0]
    match = row_tenant_index == jnp.arange(slots, dtype=jnp.int32)[None, :]
    slot = jnp.sum(jnp.where(match, tenant_adapter_slot[None, :], 0), axis=1)
    same = (slot[:, None] == slot[None, :]) & live[None, :] & (number[None, :] < number[:, None])
    place = jnp.sum(same.astype(jnp.int32), axis=1)
    target = jnp.where(live, slot * MOST + place, buffer_rows)
    hit = jnp.arange(buffer_rows, dtype=jnp.int32)[:, None] == target[None, :]
    pick = hit.astype(bf16)

    if part % LANES == 0 and proj_part % LANES == 0 and LANES % (2 * rank) == 0:
        down = adapter_down_maps.transpose(0, 2, 1).reshape(local * rank, width)
        up = adapter_up_maps.reshape(local * rank, proj)
        delta, kl_rows, down_grad, up_grad = adapters(
            pick, tokens, readout, advantage.astype(f32)[None, :], down, up, owners, shares, rank
        )
        base = jnp.dot(tokens, base_all, preferred_element_type=f32)
        return (
            (base + delta.astype(f32)).astype(bf16),
            kl_rows[0],
            down_grad.reshape(local, rank, part).transpose(0, 2, 1),
            up_grad.reshape(local, rank, proj_part),
        )

    up_all = lax.all_gather(adapter_up_maps, "dp", axis=0, tiled=True)
    up_flat = up_all.reshape(slots * rank, proj)

    send_x = jnp.stack(
        [
            jnp.dot(pick, tokens[:, i * part : (i + 1) * part], preferred_element_type=f32)
            .astype(bf16)
            .reshape(owners, per_owner, part)
            for i in range(shares)
        ],
        axis=1,
    ).reshape(peers, per_owner, part)
    x = lax.all_to_all(send_x, both, split_axis=0, concat_axis=0, tiled=True)
    x = x.reshape(peers * per_owner, part)
    at = jnp.arange(peers * per_owner, dtype=jnp.int32) % per_owner // MOST
    chosen = at[:, None] == jnp.arange(local, dtype=jnp.int32)[None, :]

    down = lax.dynamic_slice_in_dim(adapter_down_maps, share * part, part, 1)
    every = jnp.einsum("au,wuq->awq", x, down, preferred_element_type=f32)
    low_part = jnp.sum(jnp.where(chosen[:, :, None], every, 0.0), axis=1)
    low_back = lax.all_to_all(
        low_part.reshape(peers, per_owner, rank), both, split_axis=0, concat_axis=0, tiled=True
    )
    low_buffer = jnp.sum(low_back.reshape(owners, shares, per_owner, rank), axis=1)
    low_buffer = rounded(low_buffer.reshape(buffer_rows, rank))

    low = jnp.einsum("br,bq->rq", pick, low_buffer, preferred_element_type=f32).astype(bf16)
    here = (slot[:, None] == jnp.arange(slots, dtype=jnp.int32)[None, :]) & live[:, None]
    wide = jnp.where(here[:, :, None], low[:, None, :], jnp.zeros((), bf16)).reshape(rows, slots * rank)
    delta = rounded(adapter_scale * jnp.dot(wide, up_flat, preferred_element_type=f32))
    delta32 = delta.astype(f32)

    dir32 = readout.astype(f32)
    gap = jnp.sum(delta32 * dir32, axis=1)
    kl_rows = jnp.where(live, jnp.exp(-gap) + gap - 1.0, 0.0)
    coeff = jnp.where(live, kl_weight * (1.0 - jnp.exp(-gap)) - advantage.astype(f32), 0.0)
    cot = rounded(coeff[:, None] * dir32)
    back = jnp.einsum("ni,ki->nk", cot, up_flat, preferred_element_type=f32)
    back = jnp.where(here[:, :, None], back.reshape(rows, slots, rank), 0.0)
    low_grad = rounded(adapter_scale * jnp.sum(back, axis=1))

    def sent(a):
        return jnp.dot(pick, a, preferred_element_type=f32).astype(bf16)

    small = jnp.concatenate([low_grad, low], axis=1)
    small = sent(small).reshape(owners, 1, per_owner, 2 * rank)
    large = sent(cot).reshape(owners, per_owner, shares, proj_part).transpose(0, 2, 1, 3)
    packed = jnp.concatenate(
        [jnp.broadcast_to(small, (owners, shares, per_owner, 2 * rank)), large], axis=3
    ).reshape(peers, per_owner, 2 * rank + proj_part)
    got = lax.all_to_all(packed, both, split_axis=0, concat_axis=0, tiled=True)
    got = got.reshape(peers * per_owner, 2 * rank + proj_part)

    none = jnp.zeros((), bf16)
    grad_wide = jnp.where(chosen[:, :, None], got[:, None, :rank], none)
    low_wide = jnp.where(chosen[:, :, None], got[:, None, rank : 2 * rank], none)
    down_map_gradient = jnp.einsum("md,mtr->tdr", x, grad_wide, preferred_element_type=f32)
    up_map_gradient = adapter_scale * jnp.einsum(
        "mtr,me->tre", low_wide, got[:, 2 * rank :], preferred_element_type=f32
    )
    base = jnp.dot(tokens, base_all, preferred_element_type=f32)
    values = (base + delta32).astype(bf16)
    return values, kl_rows, down_map_gradient, up_map_gradient


def solution(mesh):
    everywhere = ("groups", "dp", "fsdp")
    placed = (
        P(everywhere, None),
        P(everywhere, None),
        P(),
        P(everywhere),
        P(everywhere, None),
        P(everywhere),
        P("fsdp", None),
        P("dp", None, None),
        P("dp", None, None),
    )
    return jax.shard_map(
        per_device,
        mesh=mesh,
        in_specs=placed,
        out_specs=(
            P(everywhere, None),
            P(everywhere),
            P(("groups", "dp"), "fsdp", None),
            P(("groups", "dp"), None, "fsdp"),
        ),
        check_vma=False,
    )
```

```python
import functools

import jax
import jax.numpy as jnp
from jax import lax
from jax.experimental import pallas as pl
from jax.experimental.pallas import tpu as pltpu
from jax.sharding import PartitionSpec as P

MOST = 8

adapter_scale = 2.0
kl_weight = 0.5
bf16 = jnp.bfloat16
f32 = jnp.float32
LANES = 128
PIECES = 2
ORDER = (0, 1, 3, 2)


def rounded(a):
    return lax.reduce_precision(a.astype(f32), 8, 7).astype(bf16)


def nt(a, b):
    return lax.dot_general(a, b, (((1,), (1,)), ((), ())), preferred_element_type=f32)


def tn(a, b):
    return lax.dot_general(a, b, (((0,), (0,)), ((), ())), preferred_element_type=f32)


def adapters_kernel(
    owners, shares, rank,
    pick_ref, tokens_ref, readout_ref, adv_ref, down_ref, up_ref, base_ref,
    values_ref, kl_ref, down_grad_ref, up_grad_ref,
    x_send, x_recv, low_send, low_recv, up_all, m_send, m_recv, dirs, base_all, acc,
    xs, xr, ls, lr, ms, mr, us, ur, vs, vr, bs, br,
):
    peers = owners * shares
    d, f = lax.axis_index("dp"), lax.axis_index("fsdp")
    g = lax.axis_index("groups")
    me = d * shares + f
    beside = f + 1 - 2 * lax.rem(f, 2)
    across = lax.rem(f + 2, shares)
    corner = lax.rem(beside + 2, shares)
    buffer_rows, rows = pick_ref.shape
    block = buffer_rows // owners
    wide = up_ref.shape[0]
    part = tokens_ref.shape[1] // shares
    cut = readout_ref.shape[1] // shares

    def where_is(p):
        return {"dp": p // shares, "fsdp": lax.rem(p, shares)}

    def copy(src, dst, send, recv, p):
        return pltpu.make_async_remote_copy(
            src_ref=src, dst_ref=dst, send_sem=send, recv_sem=recv,
            device_id=where_is(p), device_id_type=pl.DeviceIdType.MESH,
        )

    def x_copy(to, source):
        return copy(x_send.at[to], x_recv.at[source], xs.at[to], xr.at[source], to)

    def low_copy(to, source):
        return copy(low_send.at[to], low_recv.at[source], ls.at[to], lr.at[source], to)

    def m_copy(to, source):
        return copy(m_send.at[to], m_recv.at[source], ms.at[to], mr.at[source], to)

    def other(k):
        return lax.rem(me + k, peers)

    barrier = pltpu.get_barrier_semaphore()
    for k in range(1, peers):
        pl.semaphore_signal(
            barrier, inc=1, device_id=where_is(other(k)), device_id_type=pl.DeviceIdType.MESH
        )
    pl.semaphore_signal(
        barrier, inc=1, device_id={"groups": 1 - g}, device_id_type=pl.DeviceIdType.MESH
    )
    pl.semaphore_wait(barrier, peers)

    my_cut = pl.ds(pl.multiple_of(f * cut, LANES), cut)

    def up_copy(to_d, source):
        return copy(up_ref.at[:, my_cut], up_all.at[f, source], us.at[to_d], ur.at[source], to_d * shares + f)

    for j in range(1, owners):
        up_copy(lax.rem(d + j, owners), d).start()
    up_all[f, d] = up_ref[:, my_cut]

    for i in range(shares):
        s = lax.rem(f + i, shares)
        columns = pl.ds(pl.multiple_of(s * part, LANES), part)
        moved = jnp.dot(pick_ref[...], tokens_ref[:, columns], preferred_element_type=f32).astype(bf16)
        for o in range(owners):
            x_send[o * shares + s] = moved[o * block : (o + 1) * block]
        for j in range(owners):
            o = lax.rem(d + owners // 2 + j, owners)
            if i == 0 and j == owners - owners // 2:
                continue
            x_copy(o * shares + s, me).start()
    x_recv[me] = x_send[me]

    half = base_ref.shape[0] // 2
    piece = half // PIECES

    def rows_of(h, c):
        return pl.ds(pl.multiple_of(h * half + c * piece, 16), piece)

    def base_copy(src, shard, h, c, sem, device):
        return pltpu.make_async_remote_copy(
            src_ref=src.at[rows_of(h, c)], dst_ref=base_all.at[shard, rows_of(h, c)],
            send_sem=bs.at[sem], recv_sem=br.at[sem],
            device_id=device, device_id_type=pl.DeviceIdType.MESH,
        )

    def over_x(shard, c):
        return base_copy(base_ref, shard, g, c, c, {"fsdp": across})

    def over_y(h, c):
        return base_copy(base_all.at[across], across, h, c, PIECES + c, {"groups": 1 - g})

    def over_core(shard, h, c, sem):
        return base_copy(base_all.at[across], shard, h, c, sem, {"fsdp": beside})

    def core_near(shard, c):
        return over_core(shard, g, c, 2 * PIECES + c)

    def core_far(shard, c):
        return over_core(shard, 1 - g, c, 3 * PIECES + c)

    def core_own(shard):
        return pltpu.make_async_remote_copy(
            src_ref=base_ref, dst_ref=base_all.at[shard],
            send_sem=bs.at[4 * PIECES], recv_sem=br.at[4 * PIECES],
            device_id={"fsdp": beside}, device_id_type=pl.DeviceIdType.MESH,
        )

    for c in range(PIECES):
        over_x(f, c).start()
    core_own(f).start()

    def add_base(shard, ref, first=False):
        columns = pl.ds(pl.multiple_of(shard * part, LANES), part)
        for c in range(0, acc.shape[1], 512):
            product = jnp.dot(
                tokens_ref[:, columns], ref[:, c : c + 512], preferred_element_type=f32
            )
            acc[:, c : c + 512] = product if first else acc[:, c : c + 512] + product

    def up_on(shard, sem, to):
        return copy(up_all.at[shard], up_all.at[shard], vs.at[sem], vr.at[sem], d * shares + to)

    for j in range(1, owners):
        up_copy(d, lax.rem(d + j, owners)).wait_recv()
    up_on(f, 0, across).start()
    up_on(f, 1, beside).start()

    dirs[...] = jnp.dot(pick_ref[...], readout_ref[...], preferred_element_type=f32)
    hit = pick_ref[...].astype(f32) > 0.5
    adv = jnp.sum(jnp.where(hit, adv_ref[...], 0.0), axis=1, keepdims=True)

    my_part = pl.ds(pl.multiple_of(f * part, LANES), part)
    own = (
        lax.broadcasted_iota(jnp.int32, (block, wide), 0) // MOST
        == lax.broadcasted_iota(jnp.int32, (block, wide), 1) // rank
    )

    fold = LANES // rank * MOST

    def low_of(q):
        every = jnp.where(own, nt(x_recv[q], down_ref[:, my_part]), 0.0)
        total = every[:, :LANES]
        for n in range(1, wide // LANES):
            total = total + every[:, n * LANES : (n + 1) * LANES]
        return folded(total)

    def folded(a):
        a = a.reshape(a.shape[0] // fold, LANES // rank, MOST, LANES)
        return jnp.sum(a, axis=1).reshape(a.shape[0] * MOST, LANES)

    def unfolded(a):
        a = a.reshape(a.shape[0] // MOST, 1, MOST, LANES)
        a = jnp.concatenate([a] * (LANES // rank), axis=1)
        return a.reshape(a.shape[0] * fold, LANES)

    def low_step(q):
        x_copy(q, q).wait_recv()
        low_send[q] = low_of(q)
        low_copy(q, me).start()

    low_recv[me] = low_of(me)
    add_base(f, base_ref, first=True)
    for n, j in enumerate(ORDER):
        o = lax.rem(d + j, owners)
        for i in range(shares):
            if i or j:
                low_step(o * shares + lax.rem(f + i, shares))
        if n == 0:
            up_on(across, 0, across).wait_recv()
            up_on(across, 2, beside).start()
        if n < PIECES:
            over_x(across, n).wait_recv()
            over_y(g, n).start()
            core_near(across, n).start()

    for k in range(1, peers):
        low_copy(other(k), other(k)).wait_recv()
    for c in range(PIECES):
        over_y(1 - g, c).wait_recv()
        core_far(across, c).start()
    up_on(beside, 1, beside).wait_recv()
    up_on(corner, 2, beside).wait_recv()
    blocks = []
    for o in range(owners):
        total = low_recv[o * shares]
        for s in range(1, shares):
            total = total + low_recv[o * shares + s]
        blocks.append(unfolded(total))
    low32 = jnp.concatenate(blocks, axis=0).astype(bf16).astype(f32)
    columns = owners * wide
    mine = (
        lax.broadcasted_iota(jnp.int32, (buffer_rows, columns), 0) // MOST
        == lax.broadcasted_iota(jnp.int32, (buffer_rows, columns), 1) // rank
    )
    spread = jnp.where(mine, jnp.concatenate([low32] * (columns // LANES), axis=1), 0.0).astype(bf16)
    deltas = []
    gap = jnp.zeros((buffer_rows, 1), f32)
    for s in range(shares):
        up = up_all[s].reshape(columns, cut)
        delta = (adapter_scale * jnp.dot(spread, up, preferred_element_type=f32)).astype(bf16)
        deltas.append(delta)
        gap = gap + jnp.sum(delta.astype(f32) * dirs[:, s * cut : (s + 1) * cut], axis=1, keepdims=True)
    small = jnp.exp(-gap)
    coeff = kl_weight * (1.0 - small) - adv
    back = jnp.zeros((buffer_rows, columns), f32)
    for s in range(shares):
        cot = (coeff * dirs[:, s * cut : (s + 1) * cut]).astype(bf16)
        for o in range(owners):
            m_send[o * shares + s, :block] = cot[o * block : (o + 1) * block]
        back = back + nt(cot, up_all[s].reshape(columns, cut))
    back = jnp.where(mine, back, 0.0)
    total = back[:, :LANES]
    for n in range(1, columns // LANES):
        total = total + back[:, n * LANES : (n + 1) * LANES]
    kept = (
        lax.rem(lax.broadcasted_iota(jnp.int32, (buffer_rows, LANES), 0) // MOST, LANES // rank)
        == lax.broadcasted_iota(jnp.int32, (buffer_rows, LANES), 1) // rank
    )
    packed = jnp.concatenate(
        [folded(adapter_scale * total), folded(jnp.where(kept, low32, 0.0))], axis=1
    ).astype(bf16)
    short = packed.shape[0] // owners
    for o in range(owners):
        for s in range(shares):
            m_send[o * shares + s, block:] = packed[o * short : (o + 1) * short]
    for k in range(1, peers):
        m_copy(other(k), me).start()
    m_recv[me] = m_send[me]

    kl_ref[...] = jnp.sum(jnp.where(hit, small + gap - 1.0, 0.0), axis=0, keepdims=True)
    core_own(beside).wait_recv()
    add_base(beside, base_all.at[beside])
    add_base(across, base_all.at[across])
    for c in range(PIECES):
        core_near(corner, c).wait_recv()
        core_far(corner, c).wait_recv()
    add_base(corner, base_all.at[corner])
    for s in range(shares):
        at = slice(s * cut, (s + 1) * cut)
        values_ref[:, at] = (acc[:, at] + tn(pick_ref[...], deltas[s])).astype(bf16)

    for k in range(1, peers):
        m_copy(other(k), other(k)).wait_recv()
    got = m_recv[:, block:].astype(f32).reshape(peers * short, 2 * LANES)
    chosen = (
        lax.rem(lax.broadcasted_iota(jnp.int32, (peers * block, wide), 0), block) // MOST
        == lax.broadcasted_iota(jnp.int32, (peers * block, wide), 1) // rank
    )

    def widened(a):
        return jnp.where(chosen, jnp.concatenate([a] * (wide // LANES), axis=1), 0.0).astype(bf16)

    grad_wide = widened(unfolded(got[:, :LANES]))
    low_wide = widened(unfolded(got[:, LANES:]))
    for c in range(0, part, 256):
        down_grad_ref[:, c : c + 256] = tn(
            grad_wide, x_recv[:, :, c : c + 256].reshape(peers * block, 256)
        )
    up_grad_ref[...] = adapter_scale * tn(low_wide, m_recv[:, :block].reshape(peers * block, cut))

    for j in range(1, owners):
        up_copy(lax.rem(d + j, owners), d).wait_send()
    up_on(f, 0, across).wait_send()
    up_on(f, 1, beside).wait_send()
    up_on(across, 2, beside).wait_send()
    for c in range(PIECES):
        over_x(f, c).wait_send()
        over_y(g, c).wait_send()
        core_near(across, c).wait_send()
        core_far(across, c).wait_send()
    core_own(f).wait_send()
    for k in range(1, peers):
        x_copy(other(k), me).wait_send()
        low_copy(other(k), me).wait_send()
        m_copy(other(k), me).wait_send()


def adapters(pick, tokens, readout, adv, down, up, base, owners, shares, rank):
    buffer_rows, rows = pick.shape
    width, proj = tokens.shape[1], readout.shape[1]
    wide = up.shape[0]
    peers, block = owners * shares, buffer_rows // owners
    part, cut = width // shares, proj // shares
    low_rows = block * rank // LANES
    dma = pltpu.SemaphoreType.DMA
    return pl.pallas_call(
        functools.partial(adapters_kernel, owners, shares, rank),
        out_shape=(
            jax.ShapeDtypeStruct((rows, proj), bf16),
            jax.ShapeDtypeStruct((1, rows), f32),
            jax.ShapeDtypeStruct((wide, part), f32),
            jax.ShapeDtypeStruct((wide, cut), f32),
        ),
        in_specs=[pl.BlockSpec(memory_space=pltpu.VMEM)] * 7,
        out_specs=tuple([pl.BlockSpec(memory_space=pltpu.VMEM)] * 4),
        scratch_shapes=[
            pltpu.VMEM((peers, block, part), bf16),
            pltpu.VMEM((peers, block, part), bf16),
            pltpu.VMEM((peers, low_rows, LANES), f32),
            pltpu.VMEM((peers, low_rows, LANES), f32),
            pltpu.VMEM((shares, owners, wide, cut), bf16),
            pltpu.VMEM((peers, block + low_rows, cut), bf16),
            pltpu.VMEM((peers, block + low_rows, cut), bf16),
            pltpu.VMEM((buffer_rows, proj), f32),
            pltpu.VMEM((shares, part, proj), bf16),
            pltpu.VMEM((rows, proj), f32),
        ]
        + [dma((peers,))] * 6
        + [dma((owners,))] * 2
        + [dma((shares,))] * 2
        + [dma((4 * PIECES + 1,))] * 2,
        compiler_params=pltpu.CompilerParams(
            collective_id=0, has_side_effects=True, vmem_limit_bytes=56 * 1024 * 1024
        ),
        cost_estimate=pl.CostEstimate(
            flops=8 * 10**9, bytes_accessed=12 * 2**20, transcendentals=buffer_rows
        ),
    )(pick, tokens, readout, adv, down, up, base)


def per_device(
    tokens,
    row_tenant_index,
    tenant_adapter_slot,
    live_row_counts,
    readout,
    advantage,
    base_value_matrix,
    adapter_down_maps,
    adapter_up_maps,
):
    rows, width = tokens.shape
    proj = base_value_matrix.shape[1]
    owners = lax.axis_size("dp")
    shares = lax.axis_size("fsdp")
    local, _, rank = adapter_down_maps.shape
    slots = tenant_adapter_slot.shape[0]
    per_owner = local * MOST
    buffer_rows = owners * per_owner
    peers = owners * shares
    part = width // shares
    proj_part = proj // shares
    both = ("dp", "fsdp")
    share = lax.axis_index("fsdp")

    number = jnp.arange(rows, dtype=jnp.int32)
    live = number < live_row_counts[0]
    match = row_tenant_index == jnp.arange(slots, dtype=jnp.int32)[None, :]
    slot = jnp.sum(jnp.where(match, tenant_adapter_slot[None, :], 0), axis=1)
    same = (slot[:, None] == slot[None, :]) & live[None, :] & (number[None, :] < number[:, None])
    place = jnp.sum(same.astype(jnp.int32), axis=1)
    target = jnp.where(live, slot * MOST + place, buffer_rows)
    hit = jnp.arange(buffer_rows, dtype=jnp.int32)[:, None] == target[None, :]
    pick = hit.astype(bf16)

    fits = (
        lax.axis_size("groups") == 2
        and owners == len(ORDER)
        and shares == 4
        and part % 256 == 0
        and proj_part == 2 * LANES
        and LANES % rank == 0
        and local * rank % LANES == 0
    )
    if fits:
        down = adapter_down_maps.transpose(0, 2, 1).reshape(local * rank, width)
        up = adapter_up_maps.reshape(local * rank, proj)
        values, kl_rows, down_grad, up_grad = adapters(
            pick, tokens, readout, advantage.astype(f32)[None, :], down, up, base_value_matrix,
            owners, shares, rank,
        )
        return (
            values,
            kl_rows[0],
            down_grad.reshape(local, rank, part).transpose(0, 2, 1),
            up_grad.reshape(local, rank, proj_part),
        )

    base_all = lax.all_gather(base_value_matrix, "fsdp", axis=0, tiled=True)
    up_all = lax.all_gather(adapter_up_maps, "dp", axis=0, tiled=True)
    up_flat = up_all.reshape(slots * rank, proj)

    send_x = jnp.stack(
        [
            jnp.dot(pick, tokens[:, i * part : (i + 1) * part], preferred_element_type=f32)
            .astype(bf16)
            .reshape(owners, per_owner, part)
            for i in range(shares)
        ],
        axis=1,
    ).reshape(peers, per_owner, part)
    x = lax.all_to_all(send_x, both, split_axis=0, concat_axis=0, tiled=True)
    x = x.reshape(peers * per_owner, part)
    at = jnp.arange(peers * per_owner, dtype=jnp.int32) % per_owner // MOST
    chosen = at[:, None] == jnp.arange(local, dtype=jnp.int32)[None, :]

    down = lax.dynamic_slice_in_dim(adapter_down_maps, share * part, part, 1)
    every = jnp.einsum("au,wuq->awq", x, down, preferred_element_type=f32)
    low_part = jnp.sum(jnp.where(chosen[:, :, None], every, 0.0), axis=1)
    low_back = lax.all_to_all(
        low_part.reshape(peers, per_owner, rank), both, split_axis=0, concat_axis=0, tiled=True
    )
    low_buffer = jnp.sum(low_back.reshape(owners, shares, per_owner, rank), axis=1)
    low_buffer = rounded(low_buffer.reshape(buffer_rows, rank))

    low = jnp.einsum("br,bq->rq", pick, low_buffer, preferred_element_type=f32).astype(bf16)
    here = (slot[:, None] == jnp.arange(slots, dtype=jnp.int32)[None, :]) & live[:, None]
    wide = jnp.where(here[:, :, None], low[:, None, :], jnp.zeros((), bf16)).reshape(rows, slots * rank)
    delta = rounded(adapter_scale * jnp.dot(wide, up_flat, preferred_element_type=f32))
    delta32 = delta.astype(f32)

    dir32 = readout.astype(f32)
    gap = jnp.sum(delta32 * dir32, axis=1)
    kl_rows = jnp.where(live, jnp.exp(-gap) + gap - 1.0, 0.0)
    coeff = jnp.where(live, kl_weight * (1.0 - jnp.exp(-gap)) - advantage.astype(f32), 0.0)
    cot = rounded(coeff[:, None] * dir32)
    back = jnp.einsum("ni,ki->nk", cot, up_flat, preferred_element_type=f32)
    back = jnp.where(here[:, :, None], back.reshape(rows, slots, rank), 0.0)
    low_grad = rounded(adapter_scale * jnp.sum(back, axis=1))

    def sent(a):
        return jnp.dot(pick, a, preferred_element_type=f32).astype(bf16)

    small = jnp.concatenate([low_grad, low], axis=1)
    small = sent(small).reshape(owners, 1, per_owner, 2 * rank)
    large = sent(cot).reshape(owners, per_owner, shares, proj_part).transpose(0, 2, 1, 3)
    packed = jnp.concatenate(
        [jnp.broadcast_to(small, (owners, shares, per_owner, 2 * rank)), large], axis=3
    ).reshape(peers, per_owner, 2 * rank + proj_part)
    got = lax.all_to_all(packed, both, split_axis=0, concat_axis=0, tiled=True)
    got = got.reshape(peers * per_owner, 2 * rank + proj_part)

    none = jnp.zeros((), bf16)
    grad_wide = jnp.where(chosen[:, :, None], got[:, None, :rank], none)
    low_wide = jnp.where(chosen[:, :, None], got[:, None, rank : 2 * rank], none)
    down_map_gradient = jnp.einsum("md,mtr->tdr", x, grad_wide, preferred_element_type=f32)
    up_map_gradient = adapter_scale * jnp.einsum(
        "mtr,me->tre", low_wide, got[:, 2 * rank :], preferred_element_type=f32
    )
    base = jnp.dot(tokens, base_all, preferred_element_type=f32)
    values = (base + delta32).astype(bf16)
    return values, kl_rows, down_map_gradient, up_map_gradient


def solution(mesh):
    everywhere = ("groups", "dp", "fsdp")
    placed = (
        P(everywhere, None),
        P(everywhere, None),
        P(),
        P(everywhere),
        P(everywhere, None),
        P(everywhere),
        P("fsdp", None),
        P("dp", None, None),
        P("dp", None, None),
    )
    return jax.shard_map(
        per_device,
        mesh=mesh,
        in_specs=placed,
        out_specs=(
            P(everywhere, None),
            P(everywhere),
            P(("groups", "dp"), "fsdp", None),
            P(("groups", "dp"), None, "fsdp"),
        ),
        check_vma=False,
    )
```

```python
import functools

import jax
import jax.numpy as jnp
from jax import lax
from jax.experimental import pallas as pl
from jax.experimental.pallas import tpu as pltpu
from jax.sharding import PartitionSpec as P

MOST = 8

adapter_scale = 2.0
kl_weight = 0.5
bf16 = jnp.bfloat16
f32 = jnp.float32
LANES = 128
PIECES = 2
ORDER = (0, 1, 3, 2)


def rounded(a):
    return lax.reduce_precision(a.astype(f32), 8, 7).astype(bf16)


def nt(a, b):
    return lax.dot_general(a, b, (((1,), (1,)), ((), ())), preferred_element_type=f32)


def tn(a, b):
    return lax.dot_general(a, b, (((0,), (0,)), ((), ())), preferred_element_type=f32)


def adapters_kernel(
    owners, shares, rank,
    pick_ref, tokens_ref, readout_ref, adv_ref, down_ref, up_ref, base_ref,
    values_ref, kl_ref, down_grad_ref, up_grad_ref,
    x_send, x_recv, low_send, low_recv, up_all, m_send, m_recv, dirs, base_all, acc,
    xs, xr, ls, lr, ms, mr, us, ur, ws, wr, vs, vr, bs, br,
):
    peers = owners * shares
    d, f = lax.axis_index("dp"), lax.axis_index("fsdp")
    g = lax.axis_index("groups")
    me = d * shares + f
    beside = f + 1 - 2 * lax.rem(f, 2)
    across = lax.rem(f + 2, shares)
    corner = lax.rem(beside + 2, shares)
    buffer_rows, rows = pick_ref.shape
    block = buffer_rows // owners
    wide = up_ref.shape[0]
    part = tokens_ref.shape[1] // shares
    cut = readout_ref.shape[1] // shares

    def where_is(p):
        return {"dp": p // shares, "fsdp": lax.rem(p, shares)}

    def copy(src, dst, send, recv, p):
        return pltpu.make_async_remote_copy(
            src_ref=src, dst_ref=dst, send_sem=send, recv_sem=recv,
            device_id=where_is(p), device_id_type=pl.DeviceIdType.MESH,
        )

    def x_copy(to, source):
        return copy(x_send.at[to], x_recv.at[source], xs.at[to], xr.at[source], to)

    def low_copy(to, source):
        return copy(low_send.at[to], low_recv.at[source], ls.at[to], lr.at[source], to)

    def m_copy(to, source):
        return copy(m_send.at[to], m_recv.at[source], ms.at[to], mr.at[source], to)

    def other(k):
        return lax.rem(me + k, peers)

    barrier = pltpu.get_barrier_semaphore()
    for k in range(1, peers):
        pl.semaphore_signal(
            barrier, inc=1, device_id=where_is(other(k)), device_id_type=pl.DeviceIdType.MESH
        )
    pl.semaphore_signal(
        barrier, inc=1, device_id={"groups": 1 - g}, device_id_type=pl.DeviceIdType.MESH
    )
    pl.semaphore_wait(barrier, peers)

    my_cut = pl.ds(pl.multiple_of(f * cut, LANES), cut)

    def up_rows(h):
        return pl.ds(pl.multiple_of(h * (wide // 2), 16), wide // 2)

    def up_copy(to_d, source):
        return copy(
            up_ref.at[up_rows(g), my_cut], up_all.at[f, source, up_rows(g)],
            us.at[to_d], ur.at[source], to_d * shares + f,
        )

    def up_over_y(o, h):
        return pltpu.make_async_remote_copy(
            src_ref=up_all.at[f, o, up_rows(h)], dst_ref=up_all.at[f, o, up_rows(h)],
            send_sem=ws.at[o], recv_sem=wr.at[o],
            device_id={"groups": 1 - g}, device_id_type=pl.DeviceIdType.MESH,
        )

    for j in range(1, owners):
        up_copy(lax.rem(d + j, owners), d).start()
    up_all[f, d] = up_ref[:, my_cut]

    for i in range(shares):
        s = lax.rem(f + i, shares)
        columns = pl.ds(pl.multiple_of(s * part, LANES), part)
        moved = jnp.dot(pick_ref[...], tokens_ref[:, columns], preferred_element_type=f32).astype(bf16)
        for o in range(owners):
            x_send[o * shares + s] = moved[o * block : (o + 1) * block]
        for j in range(owners):
            o = lax.rem(d + owners // 2 + j, owners)
            if i == 0 and j == owners - owners // 2:
                continue
            x_copy(o * shares + s, me).start()
    x_recv[me] = x_send[me]

    half = base_ref.shape[0] // 2
    piece = half // PIECES

    def rows_of(h, c):
        return pl.ds(pl.multiple_of(h * half + c * piece, 16), piece)

    def base_copy(src, shard, h, c, sem, device):
        return pltpu.make_async_remote_copy(
            src_ref=src.at[rows_of(h, c)], dst_ref=base_all.at[shard, rows_of(h, c)],
            send_sem=bs.at[sem], recv_sem=br.at[sem],
            device_id=device, device_id_type=pl.DeviceIdType.MESH,
        )

    def over_x(shard, c):
        return base_copy(base_ref, shard, g, c, c, {"fsdp": across})

    def over_y(h, c):
        return base_copy(base_all.at[across], across, h, c, PIECES + c, {"groups": 1 - g})

    def over_core(shard, h, c, sem):
        return base_copy(base_all.at[across], shard, h, c, sem, {"fsdp": beside})

    def core_near(shard, c):
        return over_core(shard, g, c, 2 * PIECES + c)

    def core_far(shard, c):
        return over_core(shard, 1 - g, c, 3 * PIECES + c)

    def core_own(shard):
        return pltpu.make_async_remote_copy(
            src_ref=base_ref, dst_ref=base_all.at[shard],
            send_sem=bs.at[4 * PIECES], recv_sem=br.at[4 * PIECES],
            device_id={"fsdp": beside}, device_id_type=pl.DeviceIdType.MESH,
        )

    core_own(f).start()

    def add_base(shard, ref, first=False):
        columns = pl.ds(pl.multiple_of(shard * part, LANES), part)
        for c in range(0, acc.shape[1], 512):
            product = jnp.dot(
                tokens_ref[:, columns], ref[:, c : c + 512], preferred_element_type=f32
            )
            acc[:, c : c + 512] = product if first else acc[:, c : c + 512] + product

    def up_on(shard, sem, to):
        return copy(up_all.at[shard], up_all.at[shard], vs.at[sem], vr.at[sem], d * shares + to)

    for j in range(1, owners):
        up_copy(d, lax.rem(d + j, owners)).wait_recv()
        up_over_y(lax.rem(d + j, owners), g).start()
    for j in range(1, owners):
        up_over_y(lax.rem(d + j, owners), 1 - g).wait_recv()
    up_on(f, 0, across).start()
    up_on(f, 1, beside).start()

    dirs[...] = jnp.dot(pick_ref[...], readout_ref[...], preferred_element_type=f32)
    hit = pick_ref[...].astype(f32) > 0.5
    adv = jnp.sum(jnp.where(hit, adv_ref[...], 0.0), axis=1, keepdims=True)

    my_part = pl.ds(pl.multiple_of(f * part, LANES), part)
    own = (
        lax.rem(lax.broadcasted_iota(jnp.int32, (shares * block, wide), 0), block) // MOST
        == lax.broadcasted_iota(jnp.int32, (shares * block, wide), 1) // rank
    )

    fold = LANES // rank * MOST

    def low_of(o):
        sources = x_recv[pl.ds(o * shares, shares)].reshape(shares * block, part)
        every = nt(sources, down_ref[:, my_part])
        every = jnp.where(own, every, 0.0)
        total = every[:, :LANES]
        for n in range(1, wide // LANES):
            total = total + every[:, n * LANES : (n + 1) * LANES]
        total = folded(total)
        each = total.shape[0] // shares
        for i in range(shares):
            low_send[o * shares + i] = total[i * each : (i + 1) * each]

    def folded(a):
        a = a.reshape(a.shape[0] // fold, LANES // rank, MOST, LANES)
        return jnp.sum(a, axis=1).reshape(a.shape[0] * MOST, LANES)

    def unfolded(a):
        a = a.reshape(a.shape[0] // MOST, 1, MOST, LANES)
        a = jnp.concatenate([a] * (LANES // rank), axis=1)
        return a.reshape(a.shape[0] * fold, LANES)

    add_base(f, base_ref, first=True)
    for n, j in enumerate(ORDER):
        o = lax.rem(d + j, owners)
        turns = range(0 if j else 1, shares)
        for i in turns:
            q = o * shares + lax.rem(f + i, shares)
            x_copy(q, q).wait_recv()
        low_of(o)
        for i in turns:
            low_copy(o * shares + lax.rem(f + i, shares), me).start()
        if n == 0:
            low_recv[me] = low_send[me]
        if n == 0:
            up_on(across, 0, across).wait_recv()
            up_on(across, 2, beside).start()
            for c in range(PIECES):
                over_x(f, c).start()
        if n >= 4 - PIECES:
            c = n - 4 + PIECES
            over_x(across, c).wait_recv()
            over_y(g, c).start()
            core_near(across, c).start()

    for k in range(1, peers):
        low_copy(other(k), other(k)).wait_recv()
    for c in range(PIECES):
        over_y(1 - g, c).wait_recv()
        core_far(across, c).start()
    up_on(beside, 1, beside).wait_recv()
    up_on(corner, 2, beside).wait_recv()
    blocks = []
    for o in range(owners):
        total = low_recv[o * shares]
        for s in range(1, shares):
            total = total + low_recv[o * shares + s]
        blocks.append(unfolded(total))
    low32 = jnp.concatenate(blocks, axis=0).astype(bf16).astype(f32)
    columns = owners * wide
    mine = (
        lax.broadcasted_iota(jnp.int32, (buffer_rows, columns), 0) // MOST
        == lax.broadcasted_iota(jnp.int32, (buffer_rows, columns), 1) // rank
    )
    spread = jnp.where(mine, jnp.concatenate([low32] * (columns // LANES), axis=1), 0.0).astype(bf16)
    deltas = []
    gap = jnp.zeros((buffer_rows, 1), f32)
    for s in range(shares):
        up = up_all[s].reshape(columns, cut)
        delta = (adapter_scale * jnp.dot(spread, up, preferred_element_type=f32)).astype(bf16)
        deltas.append(delta)
        gap = gap + jnp.sum(delta.astype(f32) * dirs[:, s * cut : (s + 1) * cut], axis=1, keepdims=True)
    small = jnp.exp(-gap)
    coeff = kl_weight * (1.0 - small) - adv
    back = jnp.zeros((buffer_rows, columns), f32)
    for s in range(shares):
        cot = (coeff * dirs[:, s * cut : (s + 1) * cut]).astype(bf16)
        for o in range(owners):
            m_send[o * shares + s, :block] = cot[o * block : (o + 1) * block]
        back = back + nt(cot, up_all[s].reshape(columns, cut))
    back = jnp.where(mine, back, 0.0)
    total = back[:, :LANES]
    for n in range(1, columns // LANES):
        total = total + back[:, n * LANES : (n + 1) * LANES]
    kept = (
        lax.rem(lax.broadcasted_iota(jnp.int32, (buffer_rows, LANES), 0) // MOST, LANES // rank)
        == lax.broadcasted_iota(jnp.int32, (buffer_rows, LANES), 1) // rank
    )
    packed = jnp.concatenate(
        [folded(adapter_scale * total), folded(jnp.where(kept, low32, 0.0))], axis=1
    ).astype(bf16)
    short = packed.shape[0] // owners
    for o in range(owners):
        for s in range(shares):
            m_send[o * shares + s, block:] = packed[o * short : (o + 1) * short]
    for k in range(1, peers):
        m_copy(other(k), me).start()
    m_recv[me] = m_send[me]

    kl_ref[...] = jnp.sum(jnp.where(hit, small + gap - 1.0, 0.0), axis=0, keepdims=True)
    core_own(beside).wait_recv()
    add_base(beside, base_all.at[beside])
    add_base(across, base_all.at[across])
    for c in range(PIECES):
        core_near(corner, c).wait_recv()
        core_far(corner, c).wait_recv()
    add_base(corner, base_all.at[corner])
    for s in range(shares):
        at = slice(s * cut, (s + 1) * cut)
        values_ref[:, at] = (acc[:, at] + tn(pick_ref[...], deltas[s])).astype(bf16)

    for k in range(1, peers):
        m_copy(other(k), other(k)).wait_recv()
    got = m_recv[:, block:].astype(f32).reshape(peers * short, 2 * LANES)
    chosen = (
        lax.rem(lax.broadcasted_iota(jnp.int32, (peers * block, wide), 0), block) // MOST
        == lax.broadcasted_iota(jnp.int32, (peers * block, wide), 1) // rank
    )

    def widened(a):
        return jnp.where(chosen, jnp.concatenate([a] * (wide // LANES), axis=1), 0.0).astype(bf16)

    grad_wide = widened(unfolded(got[:, :LANES]))
    low_wide = widened(unfolded(got[:, LANES:]))
    for c in range(0, part, 256):
        down_grad_ref[:, c : c + 256] = tn(
            grad_wide, x_recv[:, :, c : c + 256].reshape(peers * block, 256)
        )
    up_grad_ref[...] = adapter_scale * tn(low_wide, m_recv[:, :block].reshape(peers * block, cut))

    for j in range(1, owners):
        up_copy(lax.rem(d + j, owners), d).wait_send()
        up_over_y(lax.rem(d + j, owners), g).wait_send()
    up_on(f, 0, across).wait_send()
    up_on(f, 1, beside).wait_send()
    up_on(across, 2, beside).wait_send()
    for c in range(PIECES):
        over_x(f, c).wait_send()
        over_y(g, c).wait_send()
        core_near(across, c).wait_send()
        core_far(across, c).wait_send()
    core_own(f).wait_send()
    for k in range(1, peers):
        x_copy(other(k), me).wait_send()
        low_copy(other(k), me).wait_send()
        m_copy(other(k), me).wait_send()


def adapters(pick, tokens, readout, adv, down, up, base, owners, shares, rank):
    buffer_rows, rows = pick.shape
    width, proj = tokens.shape[1], readout.shape[1]
    wide = up.shape[0]
    peers, block = owners * shares, buffer_rows // owners
    part, cut = width // shares, proj // shares
    low_rows = block * rank // LANES
    dma = pltpu.SemaphoreType.DMA
    return pl.pallas_call(
        functools.partial(adapters_kernel, owners, shares, rank),
        out_shape=(
            jax.ShapeDtypeStruct((rows, proj), bf16),
            jax.ShapeDtypeStruct((1, rows), f32),
            jax.ShapeDtypeStruct((wide, part), f32),
            jax.ShapeDtypeStruct((wide, cut), f32),
        ),
        in_specs=[pl.BlockSpec(memory_space=pltpu.VMEM)] * 7,
        out_specs=tuple([pl.BlockSpec(memory_space=pltpu.VMEM)] * 4),
        scratch_shapes=[
            pltpu.VMEM((peers, block, part), bf16),
            pltpu.VMEM((peers, block, part), bf16),
            pltpu.VMEM((peers, low_rows, LANES), f32),
            pltpu.VMEM((peers, low_rows, LANES), f32),
            pltpu.VMEM((shares, owners, wide, cut), bf16),
            pltpu.VMEM((peers, block + low_rows, cut), bf16),
            pltpu.VMEM((peers, block + low_rows, cut), bf16),
            pltpu.VMEM((buffer_rows, proj), f32),
            pltpu.VMEM((shares, part, proj), bf16),
            pltpu.VMEM((rows, proj), f32),
        ]
        + [dma((peers,))] * 6
        + [dma((owners,))] * 4
        + [dma((shares,))] * 2
        + [dma((4 * PIECES + 1,))] * 2,
        compiler_params=pltpu.CompilerParams(
            collective_id=0, has_side_effects=True, vmem_limit_bytes=56 * 1024 * 1024
        ),
        cost_estimate=pl.CostEstimate(
            flops=8 * 10**9, bytes_accessed=12 * 2**20, transcendentals=buffer_rows
        ),
    )(pick, tokens, readout, adv, down, up, base)


def per_device(
    tokens,
    row_tenant_index,
    tenant_adapter_slot,
    live_row_counts,
    readout,
    advantage,
    base_value_matrix,
    adapter_down_maps,
    adapter_up_maps,
):
    rows, width = tokens.shape
    proj = base_value_matrix.shape[1]
    owners = lax.axis_size("dp")
    shares = lax.axis_size("fsdp")
    local, _, rank = adapter_down_maps.shape
    slots = tenant_adapter_slot.shape[0]
    per_owner = local * MOST
    buffer_rows = owners * per_owner
    peers = owners * shares
    part = width // shares
    proj_part = proj // shares
    both = ("dp", "fsdp")
    share = lax.axis_index("fsdp")

    number = jnp.arange(rows, dtype=jnp.int32)
    live = number < live_row_counts[0]
    match = row_tenant_index == jnp.arange(slots, dtype=jnp.int32)[None, :]
    slot = jnp.sum(jnp.where(match, tenant_adapter_slot[None, :], 0), axis=1)
    same = (slot[:, None] == slot[None, :]) & live[None, :] & (number[None, :] < number[:, None])
    place = jnp.sum(same.astype(jnp.int32), axis=1)
    target = jnp.where(live, slot * MOST + place, buffer_rows)
    hit = jnp.arange(buffer_rows, dtype=jnp.int32)[:, None] == target[None, :]
    pick = hit.astype(bf16)

    fits = (
        lax.axis_size("groups") == 2
        and owners == len(ORDER)
        and shares == 4
        and part % 256 == 0
        and proj_part == 2 * LANES
        and LANES % rank == 0
        and local * rank % LANES == 0
    )
    if fits:
        down = adapter_down_maps.transpose(0, 2, 1).reshape(local * rank, width)
        up = adapter_up_maps.reshape(local * rank, proj)
        values, kl_rows, down_grad, up_grad = adapters(
            pick, tokens, readout, advantage.astype(f32)[None, :], down, up, base_value_matrix,
            owners, shares, rank,
        )
        return (
            values,
            kl_rows[0],
            down_grad.reshape(local, rank, part).transpose(0, 2, 1),
            up_grad.reshape(local, rank, proj_part),
        )

    base_all = lax.all_gather(base_value_matrix, "fsdp", axis=0, tiled=True)
    up_all = lax.all_gather(adapter_up_maps, "dp", axis=0, tiled=True)
    up_flat = up_all.reshape(slots * rank, proj)

    send_x = jnp.stack(
        [
            jnp.dot(pick, tokens[:, i * part : (i + 1) * part], preferred_element_type=f32)
            .astype(bf16)
            .reshape(owners, per_owner, part)
            for i in range(shares)
        ],
        axis=1,
    ).reshape(peers, per_owner, part)
    x = lax.all_to_all(send_x, both, split_axis=0, concat_axis=0, tiled=True)
    x = x.reshape(peers * per_owner, part)
    at = jnp.arange(peers * per_owner, dtype=jnp.int32) % per_owner // MOST
    chosen = at[:, None] == jnp.arange(local, dtype=jnp.int32)[None, :]

    down = lax.dynamic_slice_in_dim(adapter_down_maps, share * part, part, 1)
    every = jnp.einsum("au,wuq->awq", x, down, preferred_element_type=f32)
    low_part = jnp.sum(jnp.where(chosen[:, :, None], every, 0.0), axis=1)
    low_back = lax.all_to_all(
        low_part.reshape(peers, per_owner, rank), both, split_axis=0, concat_axis=0, tiled=True
    )
    low_buffer = jnp.sum(low_back.reshape(owners, shares, per_owner, rank), axis=1)
    low_buffer = rounded(low_buffer.reshape(buffer_rows, rank))

    low = jnp.einsum("br,bq->rq", pick, low_buffer, preferred_element_type=f32).astype(bf16)
    here = (slot[:, None] == jnp.arange(slots, dtype=jnp.int32)[None, :]) & live[:, None]
    wide = jnp.where(here[:, :, None], low[:, None, :], jnp.zeros((), bf16)).reshape(rows, slots * rank)
    delta = rounded(adapter_scale * jnp.dot(wide, up_flat, preferred_element_type=f32))
    delta32 = delta.astype(f32)

    dir32 = readout.astype(f32)
    gap = jnp.sum(delta32 * dir32, axis=1)
    kl_rows = jnp.where(live, jnp.exp(-gap) + gap - 1.0, 0.0)
    coeff = jnp.where(live, kl_weight * (1.0 - jnp.exp(-gap)) - advantage.astype(f32), 0.0)
    cot = rounded(coeff[:, None] * dir32)
    back = jnp.einsum("ni,ki->nk", cot, up_flat, preferred_element_type=f32)
    back = jnp.where(here[:, :, None], back.reshape(rows, slots, rank), 0.0)
    low_grad = rounded(adapter_scale * jnp.sum(back, axis=1))

    def sent(a):
        return jnp.dot(pick, a, preferred_element_type=f32).astype(bf16)

    small = jnp.concatenate([low_grad, low], axis=1)
    small = sent(small).reshape(owners, 1, per_owner, 2 * rank)
    large = sent(cot).reshape(owners, per_owner, shares, proj_part).transpose(0, 2, 1, 3)
    packed = jnp.concatenate(
        [jnp.broadcast_to(small, (owners, shares, per_owner, 2 * rank)), large], axis=3
    ).reshape(peers, per_owner, 2 * rank + proj_part)
    got = lax.all_to_all(packed, both, split_axis=0, concat_axis=0, tiled=True)
    got = got.reshape(peers * per_owner, 2 * rank + proj_part)

    none = jnp.zeros((), bf16)
    grad_wide = jnp.where(chosen[:, :, None], got[:, None, :rank], none)
    low_wide = jnp.where(chosen[:, :, None], got[:, None, rank : 2 * rank], none)
    down_map_gradient = jnp.einsum("md,mtr->tdr", x, grad_wide, preferred_element_type=f32)
    up_map_gradient = adapter_scale * jnp.einsum(
        "mtr,me->tre", low_wide, got[:, 2 * rank :], preferred_element_type=f32
    )
    base = jnp.dot(tokens, base_all, preferred_element_type=f32)
    values = (base + delta32).astype(bf16)
    return values, kl_rows, down_map_gradient, up_map_gradient


def solution(mesh):
    everywhere = ("groups", "dp", "fsdp")
    placed = (
        P(everywhere, None),
        P(everywhere, None),
        P(),
        P(everywhere),
        P(everywhere, None),
        P(everywhere),
        P("fsdp", None),
        P("dp", None, None),
        P("dp", None, None),
    )
    return jax.shard_map(
        per_device,
        mesh=mesh,
        in_specs=placed,
        out_specs=(
            P(everywhere, None),
            P(everywhere),
            P(("groups", "dp"), "fsdp", None),
            P(("groups", "dp"), None, "fsdp"),
        ),
        check_vma=False,
    )
```
